32 devices in a mesh: dp: 4 (over z), ctx: 2 (over y), tensor: 4 (over x, core).
Axes of the slice: x: 2, y: 2, z: 4, core: 2. Of those that a mesh axis runs over, the one named last changes fastest.
Arguments:
- tokens: bfloat16 [16384, 1024], P(('dp', 'ctx', 'tensor')), may hold values from -6 to 6
- segment_ids: int32 [16384], P('dp'), may hold values from 0 to 3, as said below
- w_query: bfloat16 [1024, 2048], P(('dp', 'ctx'), 'tensor'), may hold values from -0.1875 to 0.1875
- key_matrix: bfloat16 [1024, 1024], P(('dp', 'ctx'), 'tensor'), may hold values from -0.1875 to 0.1875
- value_matrix: bfloat16 [1024, 1024], P(('dp', 'ctx'), 'tensor'), may hold values from -0.1875 to 0.1875
- w_out: bfloat16 [2048, 1024], P('tensor', ('dp', 'ctx')), may hold values from -2 to 2
- w_gate: bfloat16 [1024, 3072], P(('dp', 'ctx'), 'tensor'), may hold values from -0.1875 to 0.1875
- w_up: bfloat16 [1024, 3072], P(('dp', 'ctx'), 'tensor'), may hold values from -0.1875 to 0.1875
- w_down: bfloat16 [3072, 1024], P('tensor', ('dp', 'ctx')), may hold values from -0.109375 to 0.109375
- gain_attn: bfloat16 [1024], P(('dp', 'ctx')), may hold values from 0.5 to 1.5
- gain_mlp: bfloat16 [1024], P(('dp', 'ctx')), may hold values from 0.5 to 1.5
- gain_query: bfloat16 [128], P(('dp', 'ctx')), may hold values from 0.5 to 1.5
- gain_key: bfloat16 [128], P(('dp', 'ctx')), may hold values from 0.5 to 1.5
- out_cot: bfloat16 [16384, 1024], P(('dp', 'ctx', 'tensor')), may hold values from -6 to 6
Outputs:
- layer_out: bfloat16 [16384, 1024], P(('dp', 'ctx', 'tensor'))
- d_tokens: bfloat16 [16384, 1024], P(('dp', 'ctx', 'tensor'))
- grad_w_query: float32 [1024, 2048], P(('dp', 'ctx'), 'tensor')
- grad_w_key: float32 [1024, 1024], P(('dp', 'ctx'), 'tensor')
- grad_w_value: float32 [1024, 1024], P(('dp', 'ctx'), 'tensor')
- grad_w_out: float32 [2048, 1024], P('tensor', ('dp', 'ctx'))
- grad_w_gate: float32 [1024, 3072], P(('dp', 'ctx'), 'tensor')
- grad_w_up: float32 [1024, 3072], P(('dp', 'ctx'), 'tensor')
- grad_w_down: float32 [3072, 1024], P('tensor', ('dp', 'ctx'))
- grad_gain_attn: float32 [1024], P(('dp', 'ctx'))
- grad_gain_mlp: float32 [1024], P(('dp', 'ctx'))
- grad_gain_query: float32 [128], P(('dp', 'ctx'))
- grad_gain_key: float32 [128], P(('dp', 'ctx'))
The draws below stay inside these ranges and needn't reach their ends.
Inputs may be any that keep to these rules, and one draw needn't show every extreme that they name: `segment_ids`: within each data group of 4096 tokens the ids never fall, the first token has id 0 and the last id 3; one segment holds token 2047 and token 2048 of its group.
All inputs are finite; a program needn't handle non-finite values.
Results may differ from the reference program's by a relative error of at most 0.024.
Values may be sent and summed in bfloat16 or wider, within the bound.
A program may use at most 256 MiB of HBM per device.

```python
import jax
import jax.numpy as jnp
from jax import lax

MODEL_WIDTH = 1024
FF = 3072
QUERY_HEADS = 16
KEY_VALUE_HEADS = 8
HEAD_SIZE = 128
GROUP = 4096
TOKENS = 16384


def draw_segment_ids(key, part):
    key = jax.random.fold_in(key, 7)
    groups = TOKENS // GROUP
    midpoint = GROUP // 2
    key_one, key_two, key_three = jax.random.split(key, 3)
    first = jax.random.randint(key_one, (groups, 1), 1, midpoint // 2)
    last = jax.random.randint(key_two, (groups, 1), midpoint + midpoint // 2 + 1, GROUP)
    cutoff = jax.random.randint(key_three, (groups, 1), 1, first + 1)
    columns = jnp.arange(GROUP, dtype=jnp.int32)[None, :]
    labels = (columns >= cutoff).astype(jnp.int32) + (columns >= first).astype(jnp.int32) + (columns >= last).astype(jnp.int32)
    return labels.reshape(groups * GROUP)


def levels(stream_key, extent, cuts, least, top_value):
    loudness = 1.0
    for position, shards_of in cuts:
        steps = jax.random.uniform(jax.random.fold_in(jax.random.fold_in(stream_key, 6), position), (shards_of,), jnp.float32, least / len(cuts), top_value / len(cuts))
        loudness = loudness * jnp.repeat(jnp.exp(steps), extent[position] // shards_of).reshape((-1,) + (1,) * (len(extent) - 1 - position))
    return loudness


def scatter_about(key, dims, deviation, bound, cuts=(), kind=jnp.bfloat16):
    loudness = levels(key, dims, cuts, -0.22, 0.18) if cuts else 1.0
    array = jax.random.normal(key, dims, jnp.float32) * deviation * loudness
    return jnp.minimum(jnp.maximum(array, -bound), bound).astype(kind)


def setup_inputs(seed: int = 0) -> dict:
    keys = jax.random.split(jax.random.key(seed), 15)
    return {
        "tokens": scatter_about(keys[0], (TOKENS, MODEL_WIDTH), 1.0, 6.0, ((0, 32),)),
        "segment_ids": draw_segment_ids(jax.random.fold_in(keys[14], 71), 0),
        "w_query": scatter_about(keys[2], (MODEL_WIDTH, QUERY_HEADS * HEAD_SIZE), MODEL_WIDTH ** -0.5, 0.1875, ((0, 8), (1, 4))),
        "key_matrix": scatter_about(keys[3], (MODEL_WIDTH, KEY_VALUE_HEADS * HEAD_SIZE), MODEL_WIDTH ** -0.5, 0.1875, ((0, 8), (1, 4))),
        "value_matrix": scatter_about(keys[4], (MODEL_WIDTH, KEY_VALUE_HEADS * HEAD_SIZE), MODEL_WIDTH ** -0.5, 0.1875, ((0, 8), (1, 4))),
        "w_out": scatter_about(keys[5], (QUERY_HEADS * HEAD_SIZE, MODEL_WIDTH), (QUERY_HEADS * HEAD_SIZE // 256) ** -0.5, 2.0, ((0, 4), (1, 8))),
        "w_gate": scatter_about(keys[6], (MODEL_WIDTH, FF), MODEL_WIDTH ** -0.5, 0.1875, ((0, 8), (1, 4))),
        "w_up": scatter_about(keys[7], (MODEL_WIDTH, FF), MODEL_WIDTH ** -0.5, 0.1875, ((0, 8), (1, 4))),
        "w_down": scatter_about(keys[8], (FF, MODEL_WIDTH), FF ** -0.5, 0.109375, ((0, 4), (1, 8))),
        "gain_attn": jnp.clip(1.0 + 0.1 * jax.random.normal(keys[9], (MODEL_WIDTH,), jnp.float32), 0.5, 1.5).astype(jnp.bfloat16),
        "gain_mlp": jnp.clip(1.0 + 0.1 * jax.random.normal(keys[10], (MODEL_WIDTH,), jnp.float32), 0.5, 1.5).astype(jnp.bfloat16),
        "gain_query": jnp.clip(1.0 + 0.1 * jax.random.normal(keys[11], (HEAD_SIZE,), jnp.float32), 0.5, 1.5).astype(jnp.bfloat16),
        "gain_key": jnp.clip(1.0 + 0.1 * jax.random.normal(keys[12], (HEAD_SIZE,), jnp.float32), 0.5, 1.5).astype(jnp.bfloat16),
        "out_cot": scatter_about(keys[13], (TOKENS, MODEL_WIDTH), 1.0, 6.0, ((0, 32),)),
    }


EPS = 1e-06
THETA = 1000000.0
EXACT_MODE = lax.Precision.HIGHEST

@jax.custom_vjp
def reduced_result(v):
    return lax.optimization_barrier(v.astype(jnp.bfloat16)).astype(jnp.float32)

@jax.custom_vjp
def reduced_backward(v):
    return v

def low_keep(v):
    return (reduced_result(v), None)

def low_pass(kept, grad):
    return (grad,)

def back_keep(v):
    return (v, None)

def back_low(kept, grad):
    return (reduced_result(grad),)
reduced_result.defvjp(low_keep, low_pass)
reduced_backward.defvjp(back_keep, back_low)

def norm_rows(field, gain):
    return field * lax.rsqrt(lax.optimization_barrier(jnp.mean(field * field, axis=-1, keepdims=True)) + EPS) * gain

def rotary_tables(segment):
    length_total = segment.shape[0]
    positions = jnp.arange(length_total, dtype=jnp.int32)
    begins = jnp.concatenate([jnp.ones((1,), dtype=jnp.bool_), segment[1:] != segment[:-1]])
    starts = lax.cummax(jnp.where(begins, positions, jnp.zeros_like(positions)), axis=0)
    offset = (positions - starts).astype(jnp.float32)
    frequency = THETA ** (-2.0 * jnp.arange(HEAD_SIZE // 2, dtype=jnp.float32) / HEAD_SIZE)
    angles = offset[:, None] * frequency[None, :]
    cosine_table = jnp.cos(angles)
    sine_table = jnp.sin(angles)
    return (jnp.concatenate([cosine_table, cosine_table], axis=-1), jnp.concatenate([sine_table, sine_table], axis=-1))

def rotate(field, cosine_table, sine_table):
    midpoint = field.shape[-1] // 2
    turned = jnp.concatenate([-field[..., midpoint:], field[..., :midpoint]], axis=-1)
    return field * cosine_table + turned * sine_table

def attend(query_rows, key_rows, value_rows, segment):
    length_total = query_rows.shape[0]
    block_length = min(512, length_total)
    sharing_count = QUERY_HEADS // KEY_VALUE_HEADS
    scaling = HEAD_SIZE ** (-0.5)
    positions = jnp.arange(length_total, dtype=jnp.int32)
    query_tiles = query_rows.reshape(length_total // block_length, block_length, KEY_VALUE_HEADS, sharing_count, HEAD_SIZE)
    segment_blocks = segment.reshape(length_total // block_length, block_length)
    position_blocks = positions.reshape(length_total // block_length, block_length)

    def one_block(pieces):
        query_part, segment_part, position_part = pieces
        scores = reduced_backward(jnp.einsum('qhgd,khd->hgqk', query_part, key_rows, precision=EXACT_MODE) * scaling)
        allowed = (segment_part[:, None] == segment[None, :]) & (positions[None, :] <= position_part[:, None])
        scores = jnp.where(allowed, scores, -1e+30)
        weights = reduced_result(jax.nn.softmax(scores, axis=-1))
        return jnp.einsum('hgqk,khd->qhgd', weights, value_rows, precision=EXACT_MODE)
    mixed = lax.map(jax.checkpoint(one_block), (query_tiles, segment_blocks, position_blocks))
    return mixed.reshape(length_total, QUERY_HEADS * HEAD_SIZE)

def layer_group(params, rows_in, segment):
    w_query, key_matrix, value_matrix, w_out, w_gate, w_up, w_down, gain_attn, gain_mlp, gain_query, gain_key = params
    length_total = rows_in.shape[0]
    cosine_table, sine_table = rotary_tables(segment)
    cosine_table = cosine_table[:, None, :]
    sine_table = sine_table[:, None, :]
    first_norm = reduced_result(norm_rows(rows_in, gain_attn))
    q_linear = reduced_backward(jnp.dot(first_norm, w_query, precision=EXACT_MODE)).reshape(length_total, QUERY_HEADS, HEAD_SIZE)
    key_linear = reduced_backward(jnp.dot(first_norm, key_matrix, precision=EXACT_MODE)).reshape(length_total, KEY_VALUE_HEADS, HEAD_SIZE)
    value_rows = reduced_result(reduced_backward(jnp.dot(first_norm, value_matrix, precision=EXACT_MODE))).reshape(length_total, KEY_VALUE_HEADS, HEAD_SIZE)
    query_rows = reduced_result(rotate(norm_rows(q_linear, gain_query), cosine_table, sine_table))
    key_rows = reduced_result(rotate(norm_rows(key_linear, gain_key), cosine_table, sine_table))
    mixed = reduced_result(reduced_backward(attend(query_rows, key_rows, value_rows, segment)))
    middle = rows_in + reduced_backward(jnp.dot(mixed, w_out, precision=EXACT_MODE))
    norm_two = reduced_result(norm_rows(middle, gain_mlp))
    gate_act = reduced_backward(jnp.dot(norm_two, w_gate, precision=EXACT_MODE))
    up_proj = reduced_backward(jnp.dot(norm_two, w_up, precision=EXACT_MODE))
    hidden = reduced_result(jax.nn.silu(gate_act) * up_proj)
    return middle + reduced_backward(jnp.dot(hidden, w_down, precision=EXACT_MODE))

def reference(tokens, segment_ids, w_query, key_matrix, value_matrix, w_out, w_gate, w_up, w_down, gain_attn, gain_mlp, gain_query, gain_key, out_cot):
    params = tuple((member.astype(jnp.float32) for member in (w_query, key_matrix, value_matrix, w_out, w_gate, w_up, w_down, gain_attn, gain_mlp, gain_query, gain_key)))
    inputs = tokens.astype(jnp.float32)
    groups = segment_ids.shape[0] // GROUP

    def forward(weights_all, rows_all):
        row_groups = rows_all.reshape(groups, GROUP, MODEL_WIDTH)
        segment_groups = segment_ids.reshape(groups, GROUP)

        def scan_step(carried, pieces):
            return (carried, layer_group(weights_all, pieces[0], pieces[1]))
        unused, outputs = lax.scan(scan_step, jnp.zeros((), jnp.float32), (row_groups, segment_groups))
        return outputs.reshape(groups * GROUP, MODEL_WIDTH)
    result, pullback = jax.vjp(forward, params, inputs)
    gradients, d_tokens = pullback(out_cot.astype(jnp.float32))
    return (result.astype(jnp.bfloat16), d_tokens.astype(jnp.bfloat16), gradients[0], gradients[1], gradients[2], gradients[3], gradients[4], gradients[5], gradients[6], gradients[7], gradients[8], gradients[9], gradients[10])
```

```python
import functools
import math

import jax
import jax.numpy as jnp
from jax import lax
from jax.experimental import pallas as pl
from jax.experimental.pallas import tpu as pltpu
from jax.sharding import PartitionSpec as P

HEAD_SIZE = 128


EPS = 1e-06
THETA = 1000000.0


def from_behind(shard, axis, by):
    length = lax.axis_size(axis)
    pairs = [(i, i + by) for i in range(length) if 0 <= i + by < length]
    return lax.ppermute(shard, axis, pairs)


def norm_rows(field, gain):
    return field * lax.rsqrt(jnp.mean(field * field, axis=-1, keepdims=True) + EPS) * gain


def norm_back(field, gain, incoming):
    inverse = lax.rsqrt(jnp.mean(field * field, axis=-1, keepdims=True) + EPS)
    scaled = incoming * gain
    d_field = inverse * scaled - field * (inverse * inverse * inverse) * jnp.mean(
        scaled * field, axis=-1, keepdims=True
    )
    return (d_field, incoming * field * inverse)


SCALE = HEAD_SIZE ** (-0.5)
SCALE_LOG2 = SCALE * math.log2(math.e)
D = HEAD_SIZE
ROWS_TILE = 256
BQ = 256
BK = 512


def rotary_own(segment, ctx_index, span):
    length_total = segment.shape[0]
    positions = jnp.arange(length_total, dtype=jnp.int32)
    begins = jnp.concatenate([jnp.ones((1,), dtype=jnp.bool_), segment[1:] != segment[:-1]])
    starts = lax.cummax(jnp.where(begins, positions, jnp.zeros_like(positions)), axis=0)
    starts = lax.dynamic_slice_in_dim(starts, ctx_index * span, span, 0)
    mine = ctx_index * span + jnp.arange(span, dtype=jnp.int32)
    offset = (mine - starts).astype(jnp.float32)
    frequency = THETA ** (-2.0 * jnp.arange(D // 2, dtype=jnp.float32) / D)
    angles = offset[:, None] * frequency[None, :]
    cosine = jnp.cos(angles)
    sine = jnp.sin(angles)
    return (
        jnp.concatenate([cosine, cosine], axis=-1),
        jnp.concatenate([-sine, sine], axis=-1),
        starts - (ctx_index - 1) * span,
    )


def head_back(lin, gain, e):
    inverse = lax.rsqrt(jnp.mean(lin * lin, axis=-1, keepdims=True) + EPS)
    scaled = e * gain
    d_lin = inverse * scaled - lin * (inverse * inverse * inverse) * jnp.mean(
        scaled * lin, axis=-1, keepdims=True
    )
    return d_lin, e * lin * inverse


def turn_back(z, cosine, sine):
    return z * cosine - pltpu.roll(z, D // 2, 1) * sine


def qkv_kernel(
    q_heads, kv_heads, x_ref, gain_ref, w_ref, cos_ref, sin_ref, qg_ref, kg_ref,
    n_ref, lin_ref, q_ref, kv_ref,
):
    normed = norm_rows(x_ref[...].astype(jnp.float32), gain_ref[...]).astype(jnp.bfloat16)
    n_ref[...] = normed
    lin = jnp.dot(normed, w_ref[...], preferred_element_type=jnp.float32)
    both = q_heads + kv_heads
    lin_ref[...] = lin[:, : both * D]
    cosine, sine = cos_ref[...], sin_ref[...]
    for h in range(both):
        gain = qg_ref[...] if h < q_heads else kg_ref[...]
        y = norm_rows(lin[:, h * D : (h + 1) * D], gain)
        y = (y * cosine + pltpu.roll(y, D // 2, 1) * sine).astype(jnp.bfloat16)
        if h < q_heads:
            q_ref[:, h * D : (h + 1) * D] = y
        else:
            kv_ref[:, (h - q_heads) * D : (h - q_heads + 1) * D] = y
    kv_ref[:, kv_heads * D :] = lin[:, both * D :].astype(jnp.bfloat16)


def qkv_call(x, gain, w, cosine, sine, query_gain, key_gain, q_heads, kv_heads):
    rows, width = x.shape
    row = lambda n: pl.BlockSpec((ROWS_TILE, n), lambda i: (i, 0))
    one = lambda s: pl.BlockSpec(s, lambda i: (0, 0))
    both = q_heads + kv_heads
    return pl.pallas_call(
        functools.partial(qkv_kernel, q_heads, kv_heads),
        grid=(rows // ROWS_TILE,),
        in_specs=[row(width), one((1, width)), one(w.shape), row(D), row(D), one((1, D)), one((1, D))],
        out_specs=[row(width), row(both * D), row(q_heads * D), row(2 * kv_heads * D)],
        out_shape=[
            jax.ShapeDtypeStruct((rows, width), jnp.bfloat16),
            jax.ShapeDtypeStruct((rows, both * D), jnp.float32),
            jax.ShapeDtypeStruct((rows, q_heads * D), jnp.bfloat16),
            jax.ShapeDtypeStruct((rows, 2 * kv_heads * D), jnp.bfloat16),
        ],
        compiler_params=pltpu.CompilerParams(vmem_limit_bytes=40 * 2**20),
        cost_estimate=pl.CostEstimate(
            flops=2 * rows * width * w.shape[1], bytes_accessed=rows * 12000, transcendentals=0
        ),
        name="qkv_forward",
    )(x, gain, w, cosine, sine, query_gain, key_gain)


def stack_heads(block, share):
    return jnp.concatenate([block[:, g * D : (g + 1) * D] for g in range(share)], axis=0)


def forward_kernel(
    span, share, lo_ref, late_ref, q_ref, k_ref, v_ref, st_ref, o_ref, li_ref, vext, acc
):
    i = pl.program_id(1)

    @pl.when(i == 0)
    def _():
        vext[:, :D] = v_ref[...]
        vext[:, D:] = jnp.ones_like(v_ref)

    q2 = stack_heads(q_ref[...], share)
    acc[...] = jnp.zeros_like(acc)
    first = span + i * BQ

    def step(kb, masked):
        ks = pl.multiple_of(kb * BK, BK)
        s = lax.dot_general(
            q2, k_ref[pl.ds(ks, BK), :], (((1,), (1,)), ((), ())),
            preferred_element_type=jnp.float32,
        )
        p = jnp.exp2(s * SCALE_LOG2)
        if masked:
            rows = first + lax.broadcasted_iota(jnp.int32, (BQ, BK), 0)
            cols = ks + lax.broadcasted_iota(jnp.int32, (BQ, BK), 1)
            keep = (cols <= rows) & (cols >= st_ref[:, :1])
            keep = jnp.where(keep, 1.0, 0.0)
            p = jnp.where(jnp.concatenate([keep] * share, axis=0) > 0.5, p, 0.0)
        acc[...] += jnp.dot(
            p.astype(jnp.bfloat16), vext[pl.ds(ks, BK), :], preferred_element_type=jnp.float32
        )

    def body(kb, carry):
        full = (kb * BK >= late_ref[i]) & ((kb + 1) * BK - 1 <= first)
        pl.when(full)(lambda: step(kb, False))
        pl.when(jnp.logical_not(full))(lambda: step(kb, True))
        return carry

    lax.fori_loop(lo_ref[i], (first + BQ + BK - 1) // BK, body, 0)
    inverse = 1.0 / acc[:, D:]
    out = (acc[:, :D] * inverse).astype(jnp.bfloat16)
    for g in range(share):
        o_ref[:, g * D : (g + 1) * D] = out[g * BQ : (g + 1) * BQ]
        li_ref[:, g * D : (g + 1) * D] = inverse[g * BQ : (g + 1) * BQ]


def forward_call(lo, late, q, kv_all, start_cols, kv_heads):
    span, q_width = q.shape
    share = q_width // D // kv_heads
    tile = pl.BlockSpec((BQ, share * D), lambda h, i, *_: (i, h))
    return pl.pallas_call(
        functools.partial(forward_kernel, span, share),
        grid_spec=pltpu.PrefetchScalarGridSpec(
            num_scalar_prefetch=2,
            grid=(kv_heads, span // BQ),
            in_specs=[
                tile,
                pl.BlockSpec((2 * span, D), lambda h, i, *_: (0, h)),
                pl.BlockSpec((2 * span, D), lambda h, i, *_: (0, kv_heads + h)),
                pl.BlockSpec((BQ, D), lambda h, i, *_: (i, 0)),
            ],
            out_specs=[tile, tile],
            scratch_shapes=[
                pltpu.VMEM((2 * span, 2 * D), jnp.bfloat16),
                pltpu.VMEM((share * BQ, 2 * D), jnp.float32),
            ],
        ),
        out_shape=[
            jax.ShapeDtypeStruct((span, q_width), jnp.bfloat16),
            jax.ShapeDtypeStruct((span, q_width), jnp.float32),
        ],
        compiler_params=pltpu.CompilerParams(vmem_limit_bytes=40 * 2**20),
        cost_estimate=pl.CostEstimate(
            flops=20 * span * span * q_width, bytes_accessed=20 * span * q_width,
            transcendentals=2 * span * span * q_width // D,
        ),
        name="attention_forward",
    )(lo, late, q, kv_all, kv_all, start_cols)


def backward_kernel(
    span, share, lo_ref, late_ref, q_ref, do_ref, o_ref, li_ref, lin_ref, cos_ref, sin_ref,
    st_ref, gain_ref, k_ref, v_ref, dq_ref, dk_ref, dv_ref, term_ref, dq_acc,
):
    h, i = pl.program_id(0), pl.program_id(1)

    @pl.when(i == 0)
    def _():
        dk_ref[...] = jnp.zeros_like(dk_ref)
        dv_ref[...] = jnp.zeros_like(dv_ref)

    @pl.when((i == 0) & (h == 0))
    def _():
        term_ref[...] = jnp.zeros_like(term_ref)

    q2 = stack_heads(q_ref[...], share)
    do2 = stack_heads(do_ref[...].astype(jnp.float32) * li_ref[...], share).astype(jnp.bfloat16)
    product = do2.astype(jnp.float32) * stack_heads(o_ref[...], share).astype(jnp.float32)
    delta = lax.dot_general(
        jnp.ones((8, D), jnp.float32), product, (((1,), (1,)), ((), ())),
        precision=lax.Precision.HIGHEST, preferred_element_type=jnp.float32,
    )[0:1]
    dq_acc[...] = jnp.zeros_like(dq_acc)
    first = span + i * BQ

    def step(kb, masked):
        ks = pl.multiple_of(kb * BK, BK)
        k = k_ref[pl.ds(ks, BK), :]
        s = lax.dot_general(
            k, q2, (((1,), (1,)), ((), ())), preferred_element_type=jnp.float32
        )
        p = jnp.exp2(s * SCALE_LOG2)
        if masked:
            rows = ks + lax.broadcasted_iota(jnp.int32, (BK, BQ), 0)
            cols = first + lax.broadcasted_iota(jnp.int32, (BK, BQ), 1)
            keep = (rows <= cols) & (rows >= st_ref[0:1, :])
            keep = jnp.where(keep, 1.0, 0.0)
            p = jnp.where(jnp.concatenate([keep] * share, axis=1) > 0.5, p, 0.0)
        dv_ref[pl.ds(ks, BK), :] += jnp.dot(
            p.astype(jnp.bfloat16), do2, preferred_element_type=jnp.float32
        )
        dp = lax.dot_general(
            v_ref[pl.ds(ks, BK), :], do2, (((1,), (1,)), ((), ())),
            preferred_element_type=jnp.float32,
        )
        ds = (p * (dp - delta)).astype(jnp.bfloat16)
        dk_ref[pl.ds(ks, BK), :] += jnp.dot(ds, q2, preferred_element_type=jnp.float32)
        dq_acc[...] += lax.dot_general(
            ds, k, (((0,), (0,)), ((), ())), preferred_element_type=jnp.float32
        )

    def body(kb, carry):
        full = (kb * BK >= late_ref[i]) & ((kb + 1) * BK - 1 <= first)
        pl.when(full)(lambda: step(kb, False))
        pl.when(jnp.logical_not(full))(lambda: step(kb, True))
        return carry

    lax.fori_loop(lo_ref[i], (first + BQ + BK - 1) // BK, body, 0)
    for g in range(share):
        e = turn_back(dq_acc[g * BQ : (g + 1) * BQ] * SCALE, cos_ref[...], sin_ref[...])
        d_lin, terms = head_back(lin_ref[:, g * D : (g + 1) * D], gain_ref[...], e)
        dq_ref[:, g * D : (g + 1) * D] = d_lin.astype(jnp.bfloat16)
        term_ref[0:1, :] += jnp.sum(terms, axis=0, keepdims=True)

    @pl.when(i == pl.num_programs(1) - 1)
    def _():
        dk_ref[...] = dk_ref[...] * SCALE


def backward_call(lo, late, q, d_mixed, mixed, inverse, lin, cosine, sine, start_rows, gain, kv_all, kv_heads):
    span, q_width = q.shape
    share = q_width // D // kv_heads
    tile = pl.BlockSpec((BQ, share * D), lambda h, i, *_: (i, h))
    table = pl.BlockSpec((BQ, D), lambda h, i, *_: (i, 0))
    whole = pl.BlockSpec((2 * span, D), lambda h, i, *_: (0, h))
    return pl.pallas_call(
        functools.partial(backward_kernel, span, share),
        grid_spec=pltpu.PrefetchScalarGridSpec(
            num_scalar_prefetch=2,
            grid=(kv_heads, span // BQ),
            in_specs=[
                tile, tile, tile, tile, tile, table, table,
                pl.BlockSpec((8, BQ), lambda h, i, *_: (0, i)),
                pl.BlockSpec((1, D), lambda h, i, *_: (0, 0)),
                whole,
                pl.BlockSpec((2 * span, D), lambda h, i, *_: (0, kv_heads + h)),
            ],
            out_specs=[tile, whole, whole, pl.BlockSpec((8, D), lambda h, i, *_: (0, 0))],
            scratch_shapes=[pltpu.VMEM((share * BQ, D), jnp.float32)],
        ),
        out_shape=[
            jax.ShapeDtypeStruct((span, q_width), jnp.bfloat16),
            jax.ShapeDtypeStruct((2 * span, kv_heads * D), jnp.float32),
            jax.ShapeDtypeStruct((2 * span, kv_heads * D), jnp.float32),
            jax.ShapeDtypeStruct((8, D), jnp.float32),
        ],
        compiler_params=pltpu.CompilerParams(vmem_limit_bytes=48 * 2**20),
        cost_estimate=pl.CostEstimate(
            flops=50 * span * span * q_width, bytes_accessed=40 * span * q_width,
            transcendentals=2 * span * span * q_width // D,
        ),
        name="attention_backward",
    )(lo, late, q, d_mixed, mixed, inverse, lin, cosine, sine, start_rows, gain, kv_all, kv_all)


def keys_back_kernel(kv_heads, dk_ref, dv_ref, come_ref, lin_ref, cos_ref, sin_ref, gain_ref, out_ref, term_ref):
    @pl.when(pl.program_id(0) == 0)
    def _():
        term_ref[...] = jnp.zeros_like(term_ref)

    come = come_ref[...].astype(jnp.float32)
    d_keys = dk_ref[...] + come[:, : kv_heads * D]
    out_ref[:, kv_heads * D :] = (dv_ref[...] + come[:, kv_heads * D :]).astype(jnp.bfloat16)
    for h in range(kv_heads):
        part = slice(h * D, (h + 1) * D)
        e = turn_back(d_keys[:, part], cos_ref[...], sin_ref[...])
        d_lin, terms = head_back(lin_ref[:, part], gain_ref[...], e)
        out_ref[:, part] = d_lin.astype(jnp.bfloat16)
        term_ref[0:1, :] += jnp.sum(terms, axis=0, keepdims=True)


def keys_back_call(dk_all, dv_all, come, lin, cosine, sine, gain, kv_heads):
    span = come.shape[0]
    tiles = span // ROWS_TILE
    width = kv_heads * D
    skip = (lin.shape[1] - width) // width
    later = pl.BlockSpec((ROWS_TILE, width), lambda i: (tiles + i, 0))
    table = pl.BlockSpec((ROWS_TILE, D), lambda i: (i, 0))
    return pl.pallas_call(
        functools.partial(keys_back_kernel, kv_heads),
        grid=(tiles,),
        in_specs=[
            later, later,
            pl.BlockSpec((ROWS_TILE, 2 * width), lambda i: (i, 0)),
            pl.BlockSpec((ROWS_TILE, width), lambda i: (i, skip)),
            table, table,
            pl.BlockSpec((1, D), lambda i: (0, 0)),
        ],
        out_specs=[
            pl.BlockSpec((ROWS_TILE, 2 * width), lambda i: (i, 0)),
            pl.BlockSpec((8, D), lambda i: (0, 0)),
        ],
        out_shape=[
            jax.ShapeDtypeStruct((span, 2 * width), jnp.bfloat16),
            jax.ShapeDtypeStruct((8, D), jnp.float32),
        ],
        compiler_params=pltpu.CompilerParams(vmem_limit_bytes=32 * 2**20),
        name="keys_backward",
    )(dk_all, dv_all, come, lin, cosine, sine, gain)


def rows_first(left, right):
    return lax.dot_general(
        left, right, (((0,), (0,)), ((), ())), preferred_element_type=jnp.float32
    )


def rows_last(left, right):
    return lax.dot_general(
        left, right, (((1,), (1,)), ((), ())), preferred_element_type=jnp.float32
    )


BOTH = ("dp", "ctx")


def per_device(
    tokens,
    segment_ids,
    w_query,
    key_matrix,
    value_matrix,
    w_out,
    w_gate,
    w_up,
    w_down,
    gain_attn,
    gain_mlp,
    gain_query,
    gain_key,
    out_cot,
):
    width = tokens.shape[1]
    q_width, kv_width, ff = w_query.shape[1], key_matrix.shape[1], w_gate.shape[1]
    q_heads, kv_heads = q_width // D, kv_width // D
    ctx_index = lax.axis_index("ctx")
    tokens_all = lax.all_gather(tokens, "tensor", axis=0, tiled=True)
    gains = jnp.concatenate([gain_attn, gain_mlp, gain_query, gain_key])
    per_gain = (gain_attn.shape[0], gain_mlp.shape[0], gain_query.shape[0], gain_key.shape[0])
    gains_all = lax.all_gather(gains[None, :], BOTH, axis=0, tiled=True).astype(jnp.float32)
    cuts = [0]
    for n in per_gain:
        cuts.append(cuts[-1] + n)
    attn_gain, mlp_gain, query_gain, key_gain = (
        gains_all[:, cuts[j] : cuts[j + 1]].reshape(1, -1) for j in range(4)
    )
    w_qkv = lax.all_gather(
        jnp.concatenate([w_query, key_matrix, value_matrix], axis=1), BOTH, axis=0, tiled=True
    )
    w_rest = lax.all_gather(
        jnp.concatenate([w_out.T, w_gate, w_up, w_down.T], axis=1), BOTH, axis=0, tiled=True
    )
    out_turned = w_rest[:, :q_width]
    gate_up = w_rest[:, q_width : q_width + 2 * ff]
    down_turned = w_rest[:, q_width + 2 * ff :]

    span = tokens_all.shape[0]
    cosine, sine, starts = rotary_own(segment_ids, ctx_index, span)
    lo = starts[::BQ] // BK
    late = starts[BQ - 1 :: BQ]
    start_cols = jnp.broadcast_to(starts[:, None], (span, D))
    start_rows = jnp.broadcast_to(starts[None, :], (8, span))

    norm_one_all, lin, query_rows, kv_rows = qkv_call(
        tokens_all, attn_gain, w_qkv, cosine, sine, query_gain, key_gain, q_heads, kv_heads
    )
    kv_all = jnp.concatenate([from_behind(kv_rows, "ctx", 1), kv_rows], axis=0)
    mixed, inverse = forward_call(lo, late, query_rows, kv_all, start_cols, kv_heads)

    attn_total = lax.psum_scatter(
        rows_last(mixed, out_turned).astype(jnp.bfloat16), "tensor", scatter_dimension=0, tiled=True
    ).astype(jnp.float32)
    rows_in = tokens.astype(jnp.float32)
    middle = rows_in + attn_total
    norm_two = norm_rows(middle, mlp_gain).astype(jnp.bfloat16)
    norm_two_all = lax.all_gather(norm_two, "tensor", axis=0, tiled=True)
    cot_all = lax.all_gather(out_cot, "tensor", axis=0, tiled=True)
    gate_act = jnp.dot(norm_two_all, gate_up[:, :ff], preferred_element_type=jnp.float32)
    up_proj = jnp.dot(norm_two_all, gate_up[:, ff:], preferred_element_type=jnp.float32)
    sigma_gate = jax.nn.sigmoid(gate_act)
    hidden = (gate_act * sigma_gate * up_proj).astype(jnp.bfloat16)
    d_hidden = jnp.dot(cot_all, down_turned, preferred_element_type=jnp.float32)
    d_gate = (d_hidden * up_proj * sigma_gate * (1.0 + gate_act * (1.0 - sigma_gate))).astype(
        jnp.bfloat16
    )
    d_up = (d_hidden * gate_act * sigma_gate).astype(jnp.bfloat16)
    d_both = jnp.concatenate([d_gate, d_up], axis=1)
    d_norm_two = lax.psum_scatter(
        rows_last(d_both, gate_up).astype(jnp.bfloat16), "tensor", scatter_dimension=0, tiled=True
    ).astype(jnp.float32)
    mlp_total = lax.psum_scatter(
        rows_last(hidden, down_turned).astype(jnp.bfloat16),
        "tensor",
        scatter_dimension=0,
        tiled=True,
    ).astype(jnp.float32)
    layer_out = (middle + mlp_total).astype(jnp.bfloat16)
    mlp_grads = lax.psum_scatter(
        jnp.concatenate(
            [
                rows_first(norm_two_all, d_both).astype(jnp.bfloat16),
                rows_first(cot_all, hidden).astype(jnp.bfloat16),
            ],
            axis=1,
        ),
        BOTH,
        scatter_dimension=0,
        tiled=True,
    ).astype(jnp.float32)

    d_middle_norm, mlp_terms = norm_back(middle, mlp_gain, d_norm_two)
    d_middle = out_cot.astype(jnp.float32) + d_middle_norm
    d_middle_all = lax.all_gather(d_middle.astype(jnp.bfloat16), "tensor", axis=0, tiled=True)
    d_mixed = jnp.dot(d_middle_all, out_turned, preferred_element_type=jnp.float32).astype(
        jnp.bfloat16
    )
    grad_out = lax.psum_scatter(
        rows_first(d_middle_all, mixed).astype(jnp.bfloat16), BOTH, scatter_dimension=0, tiled=True
    ).astype(jnp.float32)
    dq_low, dk_all, dv_all, query_terms = backward_call(
        lo, late, query_rows, d_mixed, mixed, inverse, lin, cosine, sine, start_rows,
        query_gain, kv_all, kv_heads,
    )
    come = from_behind(
        jnp.concatenate([dk_all[:span], dv_all[:span]], axis=1).astype(jnp.bfloat16), "ctx", -1
    )
    dkv_low, key_terms = keys_back_call(
        dk_all, dv_all, come, lin, cosine, sine, key_gain, kv_heads
    )
    d_qkv = jnp.concatenate([dq_low, dkv_low], axis=1)
    d_norm_one = lax.psum_scatter(
        rows_last(d_qkv, w_qkv).astype(jnp.bfloat16), "tensor", scatter_dimension=0, tiled=True
    ).astype(jnp.float32)
    qkv_grads = lax.psum_scatter(
        rows_first(norm_one_all, d_qkv).astype(jnp.bfloat16), BOTH, scatter_dimension=0, tiled=True
    ).astype(jnp.float32)
    d_rows_norm, attn_terms = norm_back(rows_in, attn_gain, d_norm_one)
    d_tokens = (d_middle + d_rows_norm).astype(jnp.bfloat16)
    blocks = gains_all.shape[0]
    terms = jnp.concatenate(
        [
            jnp.sum(attn_terms, axis=0).reshape(blocks, -1),
            jnp.sum(mlp_terms, axis=0).reshape(blocks, -1),
            query_terms[0].reshape(blocks, -1),
            key_terms[0].reshape(blocks, -1),
        ],
        axis=1,
    )
    terms = lax.psum(terms, ("dp", "ctx", "tensor"))
    place = lax.axis_index("dp") * lax.axis_size("ctx") + ctx_index
    terms = lax.dynamic_slice_in_dim(terms, place, 1, 0)[0]
    return (
        layer_out,
        d_tokens,
        qkv_grads[:, :q_width],
        qkv_grads[:, q_width : q_width + kv_width],
        qkv_grads[:, q_width + kv_width :],
        grad_out.T,
        mlp_grads[:, :ff],
        mlp_grads[:, ff : 2 * ff],
        mlp_grads[:, 2 * ff :].T,
        terms[cuts[0] : cuts[1]],
        terms[cuts[1] : cuts[2]],
        terms[cuts[2] : cuts[3]],
        terms[cuts[3] : cuts[4]],
    )


def solution(mesh):
    in_specs = (
        P(("dp", "ctx", "tensor"), None),
        P("dp"),
        P(("dp", "ctx"), "tensor"),
        P(("dp", "ctx"), "tensor"),
        P(("dp", "ctx"), "tensor"),
        P("tensor", ("dp", "ctx")),
        P(("dp", "ctx"), "tensor"),
        P(("dp", "ctx"), "tensor"),
        P("tensor", ("dp", "ctx")),
        P(("dp", "ctx")),
        P(("dp", "ctx")),
        P(("dp", "ctx")),
        P(("dp", "ctx")),
        P(("dp", "ctx", "tensor"), None),
    )
    out_specs = (
        P(("dp", "ctx", "tensor"), None),
        P(("dp", "ctx", "tensor"), None),
        P(("dp", "ctx"), "tensor"),
        P(("dp", "ctx"), "tensor"),
        P(("dp", "ctx"), "tensor"),
        P("tensor", ("dp", "ctx")),
        P(("dp", "ctx"), "tensor"),
        P(("dp", "ctx"), "tensor"),
        P("tensor", ("dp", "ctx")),
        P(("dp", "ctx")),
        P(("dp", "ctx")),
        P(("dp", "ctx")),
        P(("dp", "ctx")),
    )
    return jax.shard_map(
        per_device, mesh=mesh, in_specs=in_specs, out_specs=out_specs, check_vma=False
    )
```

```python
import functools
import math

import jax
import jax.numpy as jnp
from jax import lax
from jax.experimental import pallas as pl
from jax.experimental.pallas import tpu as pltpu
from jax.sharding import PartitionSpec as P

HEAD_SIZE = 128


EPS = 1e-06
THETA = 1000000.0


def from_behind(shard, axis, by):
    length = lax.axis_size(axis)
    pairs = [(i, i + by) for i in range(length) if 0 <= i + by < length]
    return lax.ppermute(shard, axis, pairs)


def norm_rows(field, gain):
    return field * lax.rsqrt(jnp.mean(field * field, axis=-1, keepdims=True) + EPS) * gain


def norm_back(field, gain, incoming):
    inverse = lax.rsqrt(jnp.mean(field * field, axis=-1, keepdims=True) + EPS)
    scaled = incoming * gain
    d_field = inverse * scaled - field * (inverse * inverse * inverse) * jnp.mean(
        scaled * field, axis=-1, keepdims=True
    )
    return (d_field, incoming * field * inverse)


SCALE = HEAD_SIZE ** (-0.5)
SCALE_LOG2 = SCALE * math.log2(math.e)
D = HEAD_SIZE
ROWS_TILE = 256
BQ = 256
BK = 512


def rotary_own(segment, ctx_index, span):
    length_total = segment.shape[0]
    positions = jnp.arange(length_total, dtype=jnp.int32)
    begins = jnp.concatenate([jnp.ones((1,), dtype=jnp.bool_), segment[1:] != segment[:-1]])
    starts = lax.cummax(jnp.where(begins, positions, jnp.zeros_like(positions)), axis=0)
    starts = lax.dynamic_slice_in_dim(starts, ctx_index * span, span, 0)
    mine = ctx_index * span + jnp.arange(span, dtype=jnp.int32)
    offset = (mine - starts).astype(jnp.float32)
    frequency = THETA ** (-2.0 * jnp.arange(D // 2, dtype=jnp.float32) / D)
    angles = offset[:, None] * frequency[None, :]
    cosine = jnp.cos(angles)
    sine = jnp.sin(angles)
    return (
        jnp.concatenate([cosine, cosine], axis=-1),
        jnp.concatenate([-sine, sine], axis=-1),
        starts - (ctx_index - 1) * span,
    )


def head_back(lin, gain, e):
    inverse = lax.rsqrt(jnp.mean(lin * lin, axis=-1, keepdims=True) + EPS)
    scaled = e * gain
    d_lin = inverse * scaled - lin * (inverse * inverse * inverse) * jnp.mean(
        scaled * lin, axis=-1, keepdims=True
    )
    return d_lin, e * lin * inverse


def turn_back(z, cosine, sine):
    return z * cosine - pltpu.roll(z, D // 2, 1) * sine


def qkv_kernel(
    q_heads, kv_heads, x_ref, gain_ref, w_ref, cos_ref, sin_ref, qg_ref, kg_ref,
    n_ref, lin_ref, q_ref, kv_ref,
):
    normed = norm_rows(x_ref[...].astype(jnp.float32), gain_ref[...]).astype(jnp.bfloat16)
    n_ref[...] = normed
    lin = jnp.dot(normed, w_ref[...], preferred_element_type=jnp.float32)
    both = q_heads + kv_heads
    lin_ref[...] = lin[:, : both * D]
    cosine, sine = cos_ref[...], sin_ref[...]
    for h in range(both):
        gain = qg_ref[...] if h < q_heads else kg_ref[...]
        y = norm_rows(lin[:, h * D : (h + 1) * D], gain)
        y = (y * cosine + pltpu.roll(y, D // 2, 1) * sine).astype(jnp.bfloat16)
        if h < q_heads:
            q_ref[:, h * D : (h + 1) * D] = y
        else:
            kv_ref[:, (h - q_heads) * D : (h - q_heads + 1) * D] = y
    kv_ref[:, kv_heads * D :] = lin[:, both * D :].astype(jnp.bfloat16)


def qkv_call(x, gain, w, cosine, sine, query_gain, key_gain, q_heads, kv_heads):
    rows, width = x.shape
    row = lambda n: pl.BlockSpec((ROWS_TILE, n), lambda i: (i, 0))
    one = lambda s: pl.BlockSpec(s, lambda i: (0, 0))
    both = q_heads + kv_heads
    return pl.pallas_call(
        functools.partial(qkv_kernel, q_heads, kv_heads),
        grid=(rows // ROWS_TILE,),
        in_specs=[row(width), one((1, width)), one(w.shape), row(D), row(D), one((1, D)), one((1, D))],
        out_specs=[row(width), row(both * D), row(q_heads * D), row(2 * kv_heads * D)],
        out_shape=[
            jax.ShapeDtypeStruct((rows, width), jnp.bfloat16),
            jax.ShapeDtypeStruct((rows, both * D), jnp.float32),
            jax.ShapeDtypeStruct((rows, q_heads * D), jnp.bfloat16),
            jax.ShapeDtypeStruct((rows, 2 * kv_heads * D), jnp.bfloat16),
        ],
        compiler_params=pltpu.CompilerParams(vmem_limit_bytes=40 * 2**20),
        cost_estimate=pl.CostEstimate(
            flops=2 * rows * width * w.shape[1], bytes_accessed=rows * 12000, transcendentals=0
        ),
        name="qkv_forward",
    )(x, gain, w, cosine, sine, query_gain, key_gain)


def stack_heads(block, share):
    return jnp.concatenate([block[:, g * D : (g + 1) * D] for g in range(share)], axis=0)


def forward_kernel(
    span, share, lo_ref, late_ref, q_ref, k_ref, v_ref, st_ref, o_ref, li_ref, vext, acc
):
    i = pl.program_id(1)

    @pl.when(i == 0)
    def _():
        vext[:, :D] = v_ref[...]
        vext[:, D:] = jnp.ones_like(v_ref)

    q2 = stack_heads(q_ref[...], share)
    acc[...] = jnp.zeros_like(acc)
    first = span + i * BQ

    def step(kb, masked):
        ks = pl.multiple_of(kb * BK, BK)
        s = lax.dot_general(
            q2, k_ref[pl.ds(ks, BK), :], (((1,), (1,)), ((), ())),
            preferred_element_type=jnp.float32,
        )
        p = jnp.exp2(s * SCALE_LOG2)
        if masked:
            rows = first + lax.broadcasted_iota(jnp.int32, (BQ, BK), 0)
            cols = ks + lax.broadcasted_iota(jnp.int32, (BQ, BK), 1)
            keep = (cols <= rows) & (cols >= st_ref[:, :1])
            keep = jnp.where(keep, 1.0, 0.0)
            p = jnp.where(jnp.concatenate([keep] * share, axis=0) > 0.5, p, 0.0)
        acc[...] += jnp.dot(
            p.astype(jnp.bfloat16), vext[pl.ds(ks, BK), :], preferred_element_type=jnp.float32
        )

    def body(kb, carry):
        full = (kb * BK >= late_ref[i]) & ((kb + 1) * BK - 1 <= first)
        pl.when(full)(lambda: step(kb, False))
        pl.when(jnp.logical_not(full))(lambda: step(kb, True))
        return carry

    lax.fori_loop(lo_ref[i], (first + BQ + BK - 1) // BK, body, 0)
    inverse = 1.0 / acc[:, D:]
    out = (acc[:, :D] * inverse).astype(jnp.bfloat16)
    for g in range(share):
        o_ref[:, g * D : (g + 1) * D] = out[g * BQ : (g + 1) * BQ]
        li_ref[:, g * D : (g + 1) * D] = inverse[g * BQ : (g + 1) * BQ]


def forward_call(lo, late, q, kv_all, start_cols, kv_heads):
    span, q_width = q.shape
    share = q_width // D // kv_heads
    tile = pl.BlockSpec((BQ, share * D), lambda h, i, *_: (i, h))
    return pl.pallas_call(
        functools.partial(forward_kernel, span, share),
        grid_spec=pltpu.PrefetchScalarGridSpec(
            num_scalar_prefetch=2,
            grid=(kv_heads, span // BQ),
            in_specs=[
                tile,
                pl.BlockSpec((2 * span, D), lambda h, i, *_: (0, h)),
                pl.BlockSpec((2 * span, D), lambda h, i, *_: (0, kv_heads + h)),
                pl.BlockSpec((BQ, D), lambda h, i, *_: (i, 0)),
            ],
            out_specs=[tile, tile],
            scratch_shapes=[
                pltpu.VMEM((2 * span, 2 * D), jnp.bfloat16),
                pltpu.VMEM((share * BQ, 2 * D), jnp.float32),
            ],
        ),
        out_shape=[
            jax.ShapeDtypeStruct((span, q_width), jnp.bfloat16),
            jax.ShapeDtypeStruct((span, q_width), jnp.float32),
        ],
        compiler_params=pltpu.CompilerParams(vmem_limit_bytes=40 * 2**20),
        cost_estimate=pl.CostEstimate(
            flops=20 * span * span * q_width, bytes_accessed=20 * span * q_width,
            transcendentals=2 * span * span * q_width // D,
        ),
        name="attention_forward",
    )(lo, late, q, kv_all, kv_all, start_cols)


def backward_kernel(
    span, share, lo_ref, late_ref, q_ref, do_ref, o_ref, li_ref, lin_ref, cos_ref, sin_ref,
    st_ref, gain_ref, k_ref, v_ref, dq_ref, dk_ref, dv_ref, term_ref, dq_acc,
):
    h, i = pl.program_id(0), pl.program_id(1)

    @pl.when(i == 0)
    def _():
        dk_ref[...] = jnp.zeros_like(dk_ref)
        dv_ref[...] = jnp.zeros_like(dv_ref)

    @pl.when((i == 0) & (h == 0))
    def _():
        term_ref[...] = jnp.zeros_like(term_ref)

    q2 = stack_heads(q_ref[...], share)
    do2 = stack_heads(do_ref[...].astype(jnp.float32) * li_ref[...], share).astype(jnp.bfloat16)
    product = do2.astype(jnp.float32) * stack_heads(o_ref[...], share).astype(jnp.float32)
    delta = lax.dot_general(
        jnp.ones((8, D), jnp.float32), product, (((1,), (1,)), ((), ())),
        precision=lax.Precision.HIGHEST, preferred_element_type=jnp.float32,
    )[0:1]
    dq_acc[...] = jnp.zeros_like(dq_acc)
    first = span + i * BQ

    def step(kb, masked):
        ks = pl.multiple_of(kb * BK, BK)
        k = k_ref[pl.ds(ks, BK), :]
        s = lax.dot_general(
            k, q2, (((1,), (1,)), ((), ())), preferred_element_type=jnp.float32
        )
        p = jnp.exp2(s * SCALE_LOG2)
        if masked:
            rows = ks + lax.broadcasted_iota(jnp.int32, (BK, BQ), 0)
            cols = first + lax.broadcasted_iota(jnp.int32, (BK, BQ), 1)
            keep = (rows <= cols) & (rows >= st_ref[0:1, :])
            keep = jnp.where(keep, 1.0, 0.0)
            p = jnp.where(jnp.concatenate([keep] * share, axis=1) > 0.5, p, 0.0)
        dv_ref[pl.ds(ks, BK), :] += jnp.dot(
            p.astype(jnp.bfloat16), do2, preferred_element_type=jnp.float32
        )
        dp = lax.dot_general(
            v_ref[pl.ds(ks, BK), :], do2, (((1,), (1,)), ((), ())),
            preferred_element_type=jnp.float32,
        )
        ds = (p * (dp - delta)).astype(jnp.bfloat16)
        dk_ref[pl.ds(ks, BK), :] += jnp.dot(ds, q2, preferred_element_type=jnp.float32)
        dq_acc[...] += lax.dot_general(
            ds, k, (((0,), (0,)), ((), ())), preferred_element_type=jnp.float32
        )

    def body(kb, carry):
        full = (kb * BK >= late_ref[i]) & ((kb + 1) * BK - 1 <= first)
        pl.when(full)(lambda: step(kb, False))
        pl.when(jnp.logical_not(full))(lambda: step(kb, True))
        return carry

    lax.fori_loop(lo_ref[i], (first + BQ + BK - 1) // BK, body, 0)
    for g in range(share):
        e = turn_back(dq_acc[g * BQ : (g + 1) * BQ] * SCALE, cos_ref[...], sin_ref[...])
        d_lin, terms = head_back(lin_ref[:, g * D : (g + 1) * D], gain_ref[...], e)
        dq_ref[:, g * D : (g + 1) * D] = d_lin.astype(jnp.bfloat16)
        term_ref[0:1, :] += jnp.sum(terms, axis=0, keepdims=True)

    @pl.when(i == pl.num_programs(1) - 1)
    def _():
        dk_ref[...] = dk_ref[...] * SCALE


def backward_call(lo, late, q, d_mixed, mixed, inverse, lin, cosine, sine, start_rows, gain, kv_all, kv_heads):
    span, q_width = q.shape
    share = q_width // D // kv_heads
    tile = pl.BlockSpec((BQ, share * D), lambda h, i, *_: (i, h))
    table = pl.BlockSpec((BQ, D), lambda h, i, *_: (i, 0))
    whole = pl.BlockSpec((2 * span, D), lambda h, i, *_: (0, h))
    return pl.pallas_call(
        functools.partial(backward_kernel, span, share),
        grid_spec=pltpu.PrefetchScalarGridSpec(
            num_scalar_prefetch=2,
            grid=(kv_heads, span // BQ),
            in_specs=[
                tile, tile, tile, tile, tile, table, table,
                pl.BlockSpec((8, BQ), lambda h, i, *_: (0, i)),
                pl.BlockSpec((1, D), lambda h, i, *_: (0, 0)),
                whole,
                pl.BlockSpec((2 * span, D), lambda h, i, *_: (0, kv_heads + h)),
            ],
            out_specs=[tile, whole, whole, pl.BlockSpec((8, D), lambda h, i, *_: (0, 0))],
            scratch_shapes=[pltpu.VMEM((share * BQ, D), jnp.float32)],
        ),
        out_shape=[
            jax.ShapeDtypeStruct((span, q_width), jnp.bfloat16),
            jax.ShapeDtypeStruct((2 * span, kv_heads * D), jnp.float32),
            jax.ShapeDtypeStruct((2 * span, kv_heads * D), jnp.float32),
            jax.ShapeDtypeStruct((8, D), jnp.float32),
        ],
        compiler_params=pltpu.CompilerParams(vmem_limit_bytes=48 * 2**20),
        cost_estimate=pl.CostEstimate(
            flops=50 * span * span * q_width, bytes_accessed=40 * span * q_width,
            transcendentals=2 * span * span * q_width // D,
        ),
        name="attention_backward",
    )(lo, late, q, d_mixed, mixed, inverse, lin, cosine, sine, start_rows, gain, kv_all, kv_all)


def keys_back_kernel(kv_heads, dk_ref, dv_ref, come_ref, lin_ref, cos_ref, sin_ref, gain_ref, out_ref, term_ref):
    @pl.when(pl.program_id(0) == 0)
    def _():
        term_ref[...] = jnp.zeros_like(term_ref)

    come = come_ref[...].astype(jnp.float32)
    d_keys = dk_ref[...] + come[:, : kv_heads * D]
    out_ref[:, kv_heads * D :] = (dv_ref[...] + come[:, kv_heads * D :]).astype(jnp.bfloat16)
    for h in range(kv_heads):
        part = slice(h * D, (h + 1) * D)
        e = turn_back(d_keys[:, part], cos_ref[...], sin_ref[...])
        d_lin, terms = head_back(lin_ref[:, part], gain_ref[...], e)
        out_ref[:, part] = d_lin.astype(jnp.bfloat16)
        term_ref[0:1, :] += jnp.sum(terms, axis=0, keepdims=True)


def keys_back_call(dk_all, dv_all, come, lin, cosine, sine, gain, kv_heads):
    span = come.shape[0]
    tiles = span // ROWS_TILE
    width = kv_heads * D
    skip = (lin.shape[1] - width) // width
    later = pl.BlockSpec((ROWS_TILE, width), lambda i: (tiles + i, 0))
    table = pl.BlockSpec((ROWS_TILE, D), lambda i: (i, 0))
    return pl.pallas_call(
        functools.partial(keys_back_kernel, kv_heads),
        grid=(tiles,),
        in_specs=[
            later, later,
            pl.BlockSpec((ROWS_TILE, 2 * width), lambda i: (i, 0)),
            pl.BlockSpec((ROWS_TILE, width), lambda i: (i, skip)),
            table, table,
            pl.BlockSpec((1, D), lambda i: (0, 0)),
        ],
        out_specs=[
            pl.BlockSpec((ROWS_TILE, 2 * width), lambda i: (i, 0)),
            pl.BlockSpec((8, D), lambda i: (0, 0)),
        ],
        out_shape=[
            jax.ShapeDtypeStruct((span, 2 * width), jnp.bfloat16),
            jax.ShapeDtypeStruct((8, D), jnp.float32),
        ],
        compiler_params=pltpu.CompilerParams(vmem_limit_bytes=32 * 2**20),
        name="keys_backward",
    )(dk_all, dv_all, come, lin, cosine, sine, gain)


def rows_first(left, right):
    return lax.dot_general(
        left, right, (((0,), (0,)), ((), ())), preferred_element_type=jnp.float32
    )


def rows_last(left, right):
    return lax.dot_general(
        left, right, (((1,), (1,)), ((), ())), preferred_element_type=jnp.float32
    )


def tensor_gather(block):
    if lax.axis_size("tensor") != 4:
        return lax.all_gather(block, "tensor", axis=0, tiled=True)
    index = lax.axis_index("tensor")
    core, chip = index % 2, index // 2
    over = lax.ppermute(block, "tensor", [(t, t ^ 2) for t in range(4)])
    near = lax.ppermute(block, "tensor", [(t, t ^ 1) for t in range(4)])
    far = lax.ppermute(over, "tensor", [(t, t ^ 1) for t in range(4)])

    def order(which, one, two):
        return jnp.where(which == 0, jnp.concatenate([one, two]), jnp.concatenate([two, one]))

    return order(chip, order(core, block, near), order(core, over, far))


def tensor_scatter(total):
    if lax.axis_size("tensor") != 4:
        return lax.psum_scatter(
            total.astype(jnp.bfloat16), "tensor", scatter_dimension=0, tiled=True
        ).astype(jnp.float32)
    index = lax.axis_index("tensor")
    core, chip = index % 2, index // 2
    rows, width = total.shape
    blocks = total.astype(jnp.bfloat16).reshape(2, 2, rows // 4, width)

    def pick(i, j):
        return lax.dynamic_slice(blocks, (i, j, 0, 0), (1, 1, rows // 4, width))[0, 0]

    near = [(t, t ^ 1) for t in range(4)]
    far_came = lax.ppermute(pick(1 - chip, 1 - core), "tensor", near)
    own_came = lax.ppermute(pick(chip, 1 - core), "tensor", near)
    far_sum = pick(1 - chip, core).astype(jnp.float32) + far_came.astype(jnp.float32)
    over = lax.ppermute(
        far_sum.astype(jnp.bfloat16), "tensor", [(t, t ^ 2) for t in range(4)]
    )
    return (
        pick(chip, core).astype(jnp.float32)
        + own_came.astype(jnp.float32)
        + over.astype(jnp.float32)
    )


BOTH = ("dp", "ctx")


def per_device(
    tokens,
    segment_ids,
    w_query,
    key_matrix,
    value_matrix,
    w_out,
    w_gate,
    w_up,
    w_down,
    gain_attn,
    gain_mlp,
    gain_query,
    gain_key,
    out_cot,
):
    width = tokens.shape[1]
    q_width, kv_width, ff = w_query.shape[1], key_matrix.shape[1], w_gate.shape[1]
    q_heads, kv_heads = q_width // D, kv_width // D
    ctx_index = lax.axis_index("ctx")
    tokens_all = tensor_gather(tokens)
    gains = jnp.concatenate([gain_attn, gain_mlp, gain_query, gain_key])
    per_gain = (gain_attn.shape[0], gain_mlp.shape[0], gain_query.shape[0], gain_key.shape[0])
    gains_all = lax.all_gather(gains[None, :], BOTH, axis=0, tiled=True).astype(jnp.float32)
    cuts = [0]
    for n in per_gain:
        cuts.append(cuts[-1] + n)
    attn_gain, mlp_gain, query_gain, key_gain = (
        gains_all[:, cuts[j] : cuts[j + 1]].reshape(1, -1) for j in range(4)
    )
    w_qkv = lax.all_gather(
        jnp.concatenate([w_query, key_matrix, value_matrix], axis=1), BOTH, axis=0, tiled=True
    )
    w_rest = lax.all_gather(
        jnp.concatenate([w_out.T, w_gate, w_up, w_down.T], axis=1), BOTH, axis=0, tiled=True
    )
    out_turned = w_rest[:, :q_width]
    gate_up = w_rest[:, q_width : q_width + 2 * ff]
    down_turned = w_rest[:, q_width + 2 * ff :]

    span = tokens_all.shape[0]
    cosine, sine, starts = rotary_own(segment_ids, ctx_index, span)
    lo = starts[::BQ] // BK
    late = starts[BQ - 1 :: BQ]
    start_cols = jnp.broadcast_to(starts[:, None], (span, D))
    start_rows = jnp.broadcast_to(starts[None, :], (8, span))

    norm_one_all, lin, query_rows, kv_rows = qkv_call(
        tokens_all, attn_gain, w_qkv, cosine, sine, query_gain, key_gain, q_heads, kv_heads
    )
    kv_all = jnp.concatenate([from_behind(kv_rows, "ctx", 1), kv_rows], axis=0)
    mixed, inverse = forward_call(lo, late, query_rows, kv_all, start_cols, kv_heads)

    attn_total = tensor_scatter(rows_last(mixed, out_turned))
    rows_in = tokens.astype(jnp.float32)
    middle = rows_in + attn_total
    norm_two = norm_rows(middle, mlp_gain).astype(jnp.bfloat16)
    norm_two_all = tensor_gather(norm_two)
    cot_all = lax.all_gather(out_cot, "tensor", axis=0, tiled=True)
    gate_act = jnp.dot(norm_two_all, gate_up[:, :ff], preferred_element_type=jnp.float32)
    up_proj = jnp.dot(norm_two_all, gate_up[:, ff:], preferred_element_type=jnp.float32)
    sigma_gate = jax.nn.sigmoid(gate_act)
    hidden = (gate_act * sigma_gate * up_proj).astype(jnp.bfloat16)
    d_hidden = jnp.dot(cot_all, down_turned, preferred_element_type=jnp.float32)
    d_gate = (d_hidden * up_proj * sigma_gate * (1.0 + gate_act * (1.0 - sigma_gate))).astype(
        jnp.bfloat16
    )
    d_up = (d_hidden * gate_act * sigma_gate).astype(jnp.bfloat16)
    d_both = jnp.concatenate([d_gate, d_up], axis=1)
    d_norm_two = tensor_scatter(rows_last(d_both, gate_up))
    mlp_part = rows_last(hidden, down_turned).astype(jnp.bfloat16)
    mlp_grads = lax.psum_scatter(
        jnp.concatenate(
            [
                rows_first(norm_two_all, d_both).astype(jnp.bfloat16),
                rows_first(cot_all, hidden).astype(jnp.bfloat16),
            ],
            axis=1,
        ),
        BOTH,
        scatter_dimension=0,
        tiled=True,
    ).astype(jnp.float32)

    d_middle_norm, mlp_terms = norm_back(middle, mlp_gain, d_norm_two)
    d_middle = out_cot.astype(jnp.float32) + d_middle_norm
    d_middle_all = tensor_gather(d_middle.astype(jnp.bfloat16))
    d_mixed = jnp.dot(d_middle_all, out_turned, preferred_element_type=jnp.float32).astype(
        jnp.bfloat16
    )
    mlp_part, d_mixed = lax.optimization_barrier((mlp_part, d_mixed))
    layer_out = (middle + tensor_scatter(mlp_part)).astype(jnp.bfloat16)
    grad_out = lax.psum_scatter(
        rows_first(d_middle_all, mixed).astype(jnp.bfloat16), BOTH, scatter_dimension=0, tiled=True
    ).astype(jnp.float32)
    dq_low, dk_all, dv_all, query_terms = backward_call(
        lo, late, query_rows, d_mixed, mixed, inverse, lin, cosine, sine, start_rows,
        query_gain, kv_all, kv_heads,
    )
    dk_all, dv_all, layer_out = lax.optimization_barrier((dk_all, dv_all, layer_out))
    come = from_behind(
        jnp.concatenate([dk_all[:span], dv_all[:span]], axis=1).astype(jnp.bfloat16), "ctx", -1
    )
    dkv_low, key_terms = keys_back_call(
        dk_all, dv_all, come, lin, cosine, sine, key_gain, kv_heads
    )
    d_qkv = jnp.concatenate([dq_low, dkv_low], axis=1)
    d_norm_one = tensor_scatter(rows_last(d_qkv, w_qkv))
    qkv_grads = lax.psum_scatter(
        rows_first(norm_one_all, d_qkv).astype(jnp.bfloat16), BOTH, scatter_dimension=0, tiled=True
    ).astype(jnp.float32)
    d_rows_norm, attn_terms = norm_back(rows_in, attn_gain, d_norm_one)
    d_tokens = (d_middle + d_rows_norm).astype(jnp.bfloat16)
    blocks = gains_all.shape[0]
    terms = jnp.concatenate(
        [
            jnp.sum(attn_terms, axis=0).reshape(blocks, -1),
            jnp.sum(mlp_terms, axis=0).reshape(blocks, -1),
            query_terms[0].reshape(blocks, -1),
            key_terms[0].reshape(blocks, -1),
        ],
        axis=1,
    )
    terms = lax.psum(terms, ("dp", "ctx", "tensor"))
    place = lax.axis_index("dp") * lax.axis_size("ctx") + ctx_index
    terms = lax.dynamic_slice_in_dim(terms, place, 1, 0)[0]
    return (
        layer_out,
        d_tokens,
        qkv_grads[:, :q_width],
        qkv_grads[:, q_width : q_width + kv_width],
        qkv_grads[:, q_width + kv_width :],
        grad_out.T,
        mlp_grads[:, :ff],
        mlp_grads[:, ff : 2 * ff],
        mlp_grads[:, 2 * ff :].T,
        terms[cuts[0] : cuts[1]],
        terms[cuts[1] : cuts[2]],
        terms[cuts[2] : cuts[3]],
        terms[cuts[3] : cuts[4]],
    )


def solution(mesh):
    in_specs = (
        P(("dp", "ctx", "tensor"), None),
        P("dp"),
        P(("dp", "ctx"), "tensor"),
        P(("dp", "ctx"), "tensor"),
        P(("dp", "ctx"), "tensor"),
        P("tensor", ("dp", "ctx")),
        P(("dp", "ctx"), "tensor"),
        P(("dp", "ctx"), "tensor"),
        P("tensor", ("dp", "ctx")),
        P(("dp", "ctx")),
        P(("dp", "ctx")),
        P(("dp", "ctx")),
        P(("dp", "ctx")),
        P(("dp", "ctx", "tensor"), None),
    )
    out_specs = (
        P(("dp", "ctx", "tensor"), None),
        P(("dp", "ctx", "tensor"), None),
        P(("dp", "ctx"), "tensor"),
        P(("dp", "ctx"), "tensor"),
        P(("dp", "ctx"), "tensor"),
        P("tensor", ("dp", "ctx")),
        P(("dp", "ctx"), "tensor"),
        P(("dp", "ctx"), "tensor"),
        P("tensor", ("dp", "ctx")),
        P(("dp", "ctx")),
        P(("dp", "ctx")),
        P(("dp", "ctx")),
        P(("dp", "ctx")),
    )
    return jax.shard_map(
        per_device, mesh=mesh, in_specs=in_specs, out_specs=out_specs, check_vma=False
    )
```
